32 devices in a mesh: groups: 2 (over y), ctx: 4 (over z), exp: 2 (over x), head: 2 (over core).
Axes of the slice: x: 2, y: 2, z: 4, core: 2. Of those that a mesh axis runs over, the one named last changes fastest.
Arguments:
- latent: bfloat16 [256, 576], P(('groups', 'ctx')), parts along dimension 0, may hold values from -5 to 5
- query: bfloat16 [256, 3072], P(('groups', 'ctx'), ('exp', 'head')), parts along dimension 0, may hold values from -30 to 30
- w_uk: bfloat16 [512, 2048], P(None, ('exp', 'head')), may hold values from -0.25 to 0.25
- w_uv: bfloat16 [512, 2048], P(None, ('exp', 'head')), may hold values from -0.25 to 0.25
- w_o: bfloat16 [2048, 3584], P(('exp', 'head'), 'ctx'), may hold values from -0.5 to 0.5
- resid: bfloat16 [256, 3584], P(('groups', 'ctx', 'exp', 'head')), parts along dimension 0, may hold values from -6 to 6
- norm_gain: float32 [3584], replicated, may hold values from 0.1 to 1.9
- w_gate: bfloat16 [4, 3584, 2048], P(('exp', 'head'), None, 'ctx'), may hold values from -0.09375 to 0.09375
- w_up: bfloat16 [4, 3584, 2048], P(('exp', 'head'), None, 'ctx'), may hold values from -0.09375 to 0.09375
- w_down: bfloat16 [4, 2048, 3584], P(('exp', 'head'), None, 'ctx'), may hold values from -0.125 to 0.125
- expert_ids: int32 [256, 2], P(('groups', 'ctx', 'exp', 'head')), parts along dimension 0, may hold values from 0 to 3, all different within a row; in each aligned block of 8 rows (0 to 7, 8 to 15, ...) at most 8 rows name the same one
- route_weights: float32 [256, 2], P(('groups', 'ctx', 'exp', 'head')), parts along dimension 0, may hold values from 0.2 to 1
Outputs:
- layer_out: bfloat16 [256, 3584], P(('groups', 'ctx', 'exp', 'head')), parts along dimension 0
The draws below stay inside these ranges and needn't reach their ends.
There are 2 independent parts, one for each index of `groups`. The reference program is written for one: setup_inputs(seed, part) draws one part's arguments, and reference() takes and returns one part's arrays. A program takes and returns all parts, laid end to end along the dimension named above; an argument that names none is the same for every part. Nothing has to cross between parts.
Inputs may be any that keep to these rules, and one draw needn't show every extreme that they name: `expert_ids`: each token names 2 different experts; within each aligned block of 8 tokens no expert is named more than 8 times, a bound that some block reaches.
All inputs are finite; a program needn't handle non-finite values.
Results may differ from the reference program's by a relative error of at most 0.014.
Values may be sent and summed in bfloat16 or wider, within the bound.
No kernel may reach another device: no remote copies, remote signals or barrier semaphores. Data moves between devices by JAX's collectives and lax.ppermute only.
A program may use at most 64 MiB of HBM per device.

```python
import math
import jax
import jax.numpy as jnp
import numpy as np
from jax import lax

D = 3584
NOPE = 128
ROPE = 64
LATENT = 512
HEAD_DEV = 4
MOE_FF = 2048
TOP = 2
TOK_DEV = 8
SEQ = 128
HEADS = 16
EXPERTS = 4
CAP = 8


def draw_latent(key, part):
    base_key = jax.random.fold_in(key, 11)
    values = jnp.clip(jax.random.normal(base_key, (SEQ, LATENT + ROPE), jnp.float32), -5.0, 5.0)
    return values.astype(jnp.bfloat16)


def draw_query(key, part):
    base_key = jax.random.fold_in(key, 13)
    head_width = NOPE + ROPE
    values = jnp.clip(jax.random.normal(base_key, (SEQ, HEADS, head_width), jnp.float32), -5.0, 5.0)
    return values.reshape(SEQ, HEADS * head_width).astype(jnp.bfloat16)


def block_scale(own_key, extent, cuts, low, top_value):
    def one(position, shards_of):
        heights = jax.random.uniform(jax.random.fold_in(jax.random.fold_in(own_key, 6), position), (shards_of,), jnp.float32, low / len(cuts), top_value / len(cuts))
        return jnp.repeat(jnp.exp(heights), extent[position] // shards_of).reshape((-1,) + (1,) * (len(extent) - position - 1))

    level = one(*cuts[0])
    for cut in cuts[1:]:
        level = level * one(*cut)
    return level


def assign_block(key, own, number, rows, count, top, reach, lean):
    ranking = jax.random.permutation(key, count)
    crowded, usual = load_shares(count, rows * top, reach, lean, True), load_shares(count, rows * top, reach, lean, False)
    places = jnp.arange(count)

    def named(tallies, turn):
        used = int((tallies > 0).sum())
        fixed = max(1, used // 4)
        passed = fixed + (places - fixed + turn * (used - fixed)) % max(1, count - fixed)
        return jnp.zeros((count,), jnp.int32).at[ranking[jnp.where(places < fixed, places, passed)]].set(jnp.asarray(tallies, jnp.int32))

    tallies = jnp.where(number % 4 == 0, named(crowded, number // 4), named(usual, number - number // 4 - 1))
    mixed = jax.random.permutation(jax.random.fold_in(own, 3), count)
    giver, taker = mixed[0:count // 2 * 2:2], mixed[1:count // 2 * 2:2]
    slack = jnp.minimum(tallies[giver] - 1, reach - tallies[taker]) // 2
    slack = jnp.where((giver == ranking[0]) | (taker == ranking[0]) | (tallies[taker] == 0), 0, jnp.maximum(slack, 0))
    passed = jax.random.randint(jax.random.fold_in(own, 4), (count // 2,), 0, 1 << 20) % (slack + 1)
    tallies = tallies.at[giver].add(-passed).at[taker].add(passed)
    members = jnp.searchsorted(jnp.cumsum(tallies), jnp.arange(rows * top), side="right").astype(jnp.int32)
    table = members.reshape(top, rows).T
    table = table[jax.random.permutation(jax.random.fold_in(own, 1), rows)]
    turn = jax.random.randint(jax.random.fold_in(own, 2), (rows, 1), 0, top)
    return jnp.take_along_axis(table, (jnp.arange(top)[None, :] + turn) % top, axis=1)


def load_shares(amount, total, limit, lean, full):
    loads = [(1 << 20) // math.isqrt(rank ** lean) + 1 for rank in range(1, amount + 1)]
    largest = limit if full else min(limit, max(-(-total // amount), total * loads[0] // sum(loads)))
    least = 1 if total - largest >= amount - 1 else 0
    given, surplus = [largest] + [least] * (amount - 1), total - largest - least * (amount - 1)
    while surplus > 0:
        candidates = [i for i in range(1, amount) if given[i] < largest] or [i for i in range(1, amount) if given[i] < limit]
        whole, budget = sum([loads[i] for i in candidates]), surplus
        for i in candidates:
            addition = min(limit - given[i], max(1, budget * loads[i] // whole), surplus)
            given[i] = given[i] + addition
            surplus = surplus - addition
    return np.array(given)


def centred(own_key, extent, spread, most, shards=(), kind=jnp.bfloat16):
    result = spread * jax.random.normal(own_key, extent, jnp.float32)
    if shards:
        result = result * block_scale(own_key, extent, shards, -0.22, 0.18)
    return jnp.clip(result, -most, most).astype(kind)


def setup_inputs(seed: int = 0, part: int = 0) -> dict:
    arg_keys = jax.random.split(jax.random.key(seed), 13)
    own_keys = jax.random.split(jax.random.fold_in(arg_keys[12], part), 13)
    latent = draw_latent(jax.random.fold_in(jax.random.fold_in(arg_keys[12], part), 71), part)
    query = draw_query(jax.random.fold_in(jax.random.fold_in(arg_keys[12], part), 71), part)
    w_uk = centred(arg_keys[2], (LATENT, HEADS * NOPE), LATENT ** -0.5, 0.25, ((1, 4),))
    w_uv = centred(arg_keys[3], (LATENT, HEADS * NOPE), LATENT ** -0.5, 0.25, ((1, 4),))
    w_o = centred(arg_keys[4], (HEADS * NOPE, D), (HEADS * NOPE // 16) ** -0.5, 0.5, ((0, 4), (1, 4)))
    resid = centred(own_keys[5], (SEQ, D), 1.0, 6.0, ((0, 16),))
    norm_gain = jnp.clip(1.0 + 0.18 * jax.random.normal(arg_keys[6], (D,), jnp.float32), 0.1, 1.9)
    w_gate = centred(arg_keys[7], (EXPERTS, D, MOE_FF), D ** -0.5, 0.09375, ((0, 4), (2, 4)))
    w_up = centred(arg_keys[8], (EXPERTS, D, MOE_FF), D ** -0.5, 0.09375, ((0, 4), (2, 4)))
    w_down = centred(arg_keys[9], (EXPERTS, MOE_FF, D), MOE_FF ** -0.5, 0.125, ((0, 4), (2, 4)))
    expert_ids_keys = jax.random.split(jax.random.fold_in(own_keys[10], 1), SEQ // TOK_DEV)
    expert_ids_turns = jax.random.permutation(jax.random.fold_in(own_keys[10], 3), SEQ // TOK_DEV)
    expert_ids = jax.vmap(lambda own, number: assign_block(jax.random.fold_in(own_keys[10], 2), own, number, TOK_DEV, EXPERTS, TOP, CAP, 2))(expert_ids_keys, expert_ids_turns).reshape((SEQ, TOP))
    route_weights = jnp.clip(0.2 + 0.8 * jax.random.uniform(own_keys[11], (SEQ, TOP), jnp.float32) ** block_scale(own_keys[11], (SEQ, TOP), ((0, 16),), -0.2, 0.2), 0.2, 1.0)
    return dict(latent=latent, query=query, w_uk=w_uk, w_uv=w_uv, w_o=w_o, resid=resid, norm_gain=norm_gain, w_gate=w_gate, w_up=w_up, w_down=w_down, expert_ids=expert_ids, route_weights=route_weights)


def reference(latent, query, w_uk, w_uv, w_o, resid, norm_gain, w_gate, w_up, w_down, expert_ids, route_weights):
    compressed = latent[:, :LATENT]
    rope_keys = latent[:, LATENT:]
    head_width = NOPE + ROPE
    score_scale = 1.0 / math.sqrt(head_width)
    positions = jnp.arange(SEQ, dtype=jnp.int32)
    allowed = positions[None, :] <= positions[:, None]

    def one_head(unpack):
        query_head, key_proj, value_proj = unpack
        keys_nope = jnp.dot(compressed, key_proj, preferred_element_type=jnp.float32).astype(jnp.bfloat16)
        values_up = jnp.dot(compressed, value_proj, preferred_element_type=jnp.float32).astype(jnp.bfloat16)
        scores = jnp.dot(query_head[:, :NOPE], keys_nope.T, preferred_element_type=jnp.float32)
        scores = (scores + jnp.dot(query_head[:, NOPE:], rope_keys.T, preferred_element_type=jnp.float32)) * score_scale
        largest = lax.optimization_barrier(jnp.max(jnp.where(allowed, scores, -1e+30), axis=1, keepdims=True))
        exponent = jnp.where(allowed, jnp.exp(scores - largest), 0.0)
        probs = exponent.astype(jnp.bfloat16)
        summed = jnp.dot(probs, values_up, preferred_element_type=jnp.float32)
        return (summed / lax.optimization_barrier(jnp.sum(exponent, axis=1, keepdims=True))).astype(jnp.bfloat16)
    query_heads = query.reshape(SEQ, HEADS, head_width).transpose(1, 0, 2)
    key_heads = w_uk.reshape(LATENT, HEADS, NOPE).transpose(1, 0, 2)
    value_heads = w_uv.reshape(LATENT, HEADS, NOPE).transpose(1, 0, 2)
    per_head = lax.map(one_head, (query_heads, key_heads, value_heads))
    attended = per_head.transpose(1, 0, 2).reshape(SEQ, HEADS * NOPE)
    group_count = HEADS // HEAD_DEV
    group_width = HEAD_DEV * NOPE
    attended_groups = attended.reshape(SEQ, group_count, group_width).transpose(1, 0, 2)
    weight_groups = w_o.reshape(group_count, group_width, D)

    def add_group(total, unpack):
        rows, weights = unpack
        head_part = jnp.dot(rows, weights, preferred_element_type=jnp.float32).astype(jnp.bfloat16)
        head_part = lax.optimization_barrier(head_part)
        return (total + head_part.astype(jnp.float32), None)
    projected, unused = lax.scan(add_group, jnp.zeros((SEQ, D), jnp.float32), (attended_groups, weight_groups))
    residual_sum = resid.astype(jnp.float32) + projected
    inverse_rms = lax.rsqrt(lax.optimization_barrier(jnp.mean(residual_sum * residual_sum, axis=1, keepdims=True)) + 1e-06)
    normalized = (residual_sum * inverse_rms * norm_gain).astype(jnp.bfloat16)
    blocks = SEQ // TOK_DEV
    route_count = TOK_DEV * TOP
    block_ids = expert_ids.reshape(blocks, route_count)
    onehot = (block_ids[:, :, None] == jnp.arange(EXPERTS, dtype=jnp.int32)[None, None, :]).astype(jnp.int32)
    slot_rank = lax.optimization_barrier(jnp.sum((jnp.cumsum(onehot, axis=1) - onehot) * onehot, axis=2)).astype(jnp.int32)
    block_index = jnp.arange(blocks, dtype=jnp.int32)[:, None]
    token_index = (block_index * TOK_DEV + jnp.arange(route_count, dtype=jnp.int32)[None, :] // TOP).astype(jnp.int32)
    slot_table = jnp.full((blocks, EXPERTS, CAP), SEQ, jnp.int32)
    slot_table = slot_table.at[jnp.broadcast_to(block_index, (blocks, route_count)), block_ids, slot_rank].set(token_index)
    padded = jnp.concatenate([normalized, jnp.zeros((1, D), normalized.dtype)], axis=0)

    def one_expert(unpack):
        row_ids, gate_proj, up_proj, down_proj = unpack
        inputs = padded[row_ids]
        gate_part = jnp.dot(inputs, gate_proj, preferred_element_type=jnp.float32)
        up_part = jnp.dot(inputs, up_proj, preferred_element_type=jnp.float32)
        expert_hidden = (jax.nn.silu(gate_part) * up_part).astype(jnp.bfloat16)
        return jnp.dot(expert_hidden, down_proj, preferred_element_type=jnp.float32).astype(jnp.bfloat16)
    expert_rows = slot_table.transpose(1, 0, 2).reshape(EXPERTS, blocks * CAP)
    expert_out = lax.map(one_expert, (expert_rows, w_gate, w_up, w_down))
    flat_out = expert_out.reshape(EXPERTS * blocks * CAP, D)
    locate = (block_ids * (blocks * CAP) + block_index * CAP + slot_rank).reshape(SEQ, TOP).astype(jnp.int32)
    picked = flat_out[locate].astype(jnp.float32)
    moe_sum = lax.optimization_barrier(jnp.sum(route_weights[:, :, None] * picked, axis=1))
    return (residual_sum + moe_sum).astype(jnp.bfloat16)
```

```python
import math

import jax
import jax.numpy as jnp
from jax import lax
from jax.sharding import PartitionSpec as P

NOPE = 128
ROPE = 64
LATENT = 512
EH = ("exp", "head")
F32 = jnp.float32
BF16 = jnp.bfloat16


def send(value, axis, step):
    size = lax.axis_size(axis)
    return lax.ppermute(value, axis, [(i, (i + step) % size) for i in range(size)])


def ordered(pieces, me):
    size = len(pieces)
    stacked = jnp.stack(pieces)
    return [
        lax.dynamic_index_in_dim(stacked, (me - b) % size, 0, keepdims=False) for b in range(size)
    ]


def attend(query, latent, w_uk, w_uv, block_ids, qblock):
    rows = query.shape[0]
    head_width = NOPE + ROPE
    heads = query.shape[1] // head_width
    scale = 1.0 / math.sqrt(head_width)
    pos = (block_ids[:, None] * qblock + jnp.arange(qblock, dtype=jnp.int32)[None, :]).reshape(-1)
    compressed, rope_keys = latent[:, :LATENT], latent[:, LATENT:]
    keys = jnp.dot(compressed, w_uk, preferred_element_type=F32).astype(BF16)
    values = jnp.dot(compressed, w_uv, preferred_element_type=F32).astype(BF16)

    def part(query_rows, query_pos):
        allowed = pos[None, :] <= query_pos[:, None]
        out = []
        for h in range(heads):
            q = query_rows[:, h * head_width : (h + 1) * head_width]
            k = keys[:, h * NOPE : (h + 1) * NOPE]
            scores = jnp.einsum("qd,kd->qk", q[:, :NOPE], k, preferred_element_type=F32)
            scores = scores + jnp.einsum(
                "qd,kd->qk", q[:, NOPE:], rope_keys, preferred_element_type=F32
            )
            scores = jnp.where(allowed, scores * scale, -1e30)
            top = jnp.max(scores, axis=1, keepdims=True)
            exponent = jnp.where(allowed, jnp.exp(scores - top), 0.0)
            total = jnp.sum(exponent, axis=1, keepdims=True)
            summed = jnp.dot(
                exponent.astype(BF16),
                values[:, h * NOPE : (h + 1) * NOPE],
                preferred_element_type=F32,
            )
            out.append((summed / total).astype(BF16))
        return jnp.concatenate(out, axis=1)

    tile = rows if rows <= 256 else 128
    if tile == rows:
        return part(query, pos)
    done = lax.map(
        lambda a: part(*a), (query.reshape(-1, tile, query.shape[1]), pos.reshape(-1, tile))
    )
    return done.reshape(rows, heads * NOPE)


def shards(
    latent,
    query,
    w_uk,
    w_uv,
    w_o,
    resid,
    norm_gain,
    w_gate,
    w_up,
    w_down,
    expert_ids,
    route_weights,
):
    ctx = lax.axis_size("ctx")
    groups = lax.axis_size(EH)
    me = lax.axis_index("ctx")
    mine = lax.axis_index(EH)
    qblock = query.shape[0]
    tok = resid.shape[0]
    cols = w_o.shape[1]
    width = resid.shape[1]
    ff = w_gate.shape[2]

    packed = jnp.concatenate([query, latent], axis=1)
    pieces = [packed] + [send(packed, "ctx", d) for d in range(1, ctx)]

    experts = jnp.arange(groups, dtype=jnp.int32)
    dense = jnp.sum(
        jnp.where(expert_ids[:, :, None] == experts, route_weights[:, :, None], 0.0), axis=1
    )
    resid_cols = resid.reshape(tok, ctx, cols).transpose(1, 0, 2)
    resid_parts, dense_parts = [], []
    for d in range(ctx):
        part = lax.dynamic_index_in_dim(resid_cols, (me + d) % ctx, 0, keepdims=False)
        resid_parts.append(send(part, "ctx", d) if d else part)
        dense_parts.append(send(dense, "ctx", d) if d else dense)

    gathered = jnp.concatenate(pieces, axis=0)
    block_ids = (me - jnp.arange(ctx, dtype=jnp.int32)) % ctx
    attended = attend(
        gathered[:, : query.shape[1]],
        gathered[:, query.shape[1] :],
        w_uk,
        w_uv,
        block_ids,
        qblock,
    )
    partial = jnp.dot(attended, w_o, preferred_element_type=F32).astype(BF16)
    partial = partial.reshape(ctx, groups, tok, cols)
    total = 0.0
    for s in range(groups):
        part = lax.dynamic_index_in_dim(partial, (mine + s) % groups, 1, keepdims=False)
        total = total + (send(part, EH, s) if s else part).astype(F32)
    total = total + jnp.stack(resid_parts).astype(F32)
    residual_sum = jnp.stack(ordered([total[d] for d in range(ctx)], me))
    dense_rows = jnp.concatenate(ordered(dense_parts, me), axis=0)

    travelling = residual_sum.astype(BF16).reshape(ctx * tok, cols)
    columns = [travelling] + [send(travelling, "ctx", d) for d in range(1, ctx)]
    rows = jnp.concatenate(ordered(columns, me), axis=1).astype(F32)
    inverse_rms = lax.rsqrt(jnp.mean(rows * rows, axis=1, keepdims=True) + 1e-06)
    normalized = (rows * inverse_rms * norm_gain).astype(BF16)
    everything = lax.all_gather(normalized, EH, axis=0, tiled=True)

    gate_part = jnp.dot(everything, w_gate[0], preferred_element_type=F32)
    up_part = jnp.dot(everything, w_up[0], preferred_element_type=F32)
    hidden = (jax.nn.silu(gate_part) * up_part).astype(BF16)
    hidden = [hidden] + [send(hidden, "ctx", d) for d in range(1, ctx)]
    hidden = jnp.concatenate(ordered(hidden, me), axis=1)
    expert_cols = jnp.dot(hidden, w_down[0], preferred_element_type=F32).astype(BF16)
    expert_cols = expert_cols.reshape(groups, ctx * tok, cols)
    moe = 0.0
    for s in range(groups):
        part = lax.dynamic_index_in_dim(expert_cols, (mine + s) % groups, 0, keepdims=False)
        part = (send(part, EH, s) if s else part).astype(F32)
        weight = lax.dynamic_slice_in_dim(dense_rows, (mine - s) % groups, 1, axis=1)
        moe = moe + part * weight
    final = (residual_sum.reshape(ctx * tok, cols) + moe).astype(BF16).reshape(ctx, tok, cols)
    out = []
    for d in range(ctx):
        part = lax.dynamic_index_in_dim(final, (me + d) % ctx, 0, keepdims=False)
        out.append(send(part, "ctx", d) if d else part)
    return jnp.concatenate(ordered(out, me), axis=1)


def solution(mesh):
    placed = (
        P(("groups", "ctx"), None),
        P(("groups", "ctx"), ("exp", "head")),
        P(None, ("exp", "head")),
        P(None, ("exp", "head")),
        P(("exp", "head"), "ctx"),
        P(("groups", "ctx", "exp", "head"), None),
        P(),
        P(("exp", "head"), None, "ctx"),
        P(("exp", "head"), None, "ctx"),
        P(("exp", "head"), None, "ctx"),
        P(("groups", "ctx", "exp", "head"), None),
        P(("groups", "ctx", "exp", "head"), None),
    )
    return jax.shard_map(
        shards,
        mesh=mesh,
        in_specs=placed,
        out_specs=P(("groups", "ctx", "exp", "head"), None),
        check_vma=False,
    )
```

```python
import functools
import math

import jax
import jax.numpy as jnp
from jax import lax
from jax.experimental import pallas as pl
from jax.experimental.pallas import tpu as pltpu
from jax.sharding import PartitionSpec as P

NOPE = 128
ROPE = 64
LATENT = 512
EH = ("exp", "head")
F32 = jnp.float32
BF16 = jnp.bfloat16


def send(value, axis, step):
    size = lax.axis_size(axis)
    return lax.ppermute(value, axis, [(i, (i + step) % size) for i in range(size)])


def ordered(pieces, me):
    size = len(pieces)
    stacked = jnp.stack(pieces)
    return [
        lax.dynamic_index_in_dim(stacked, (me - b) % size, 0, keepdims=False) for b in range(size)
    ]


def attend(query, latent, w_uk, w_uv, block_ids, qblock):
    rows = query.shape[0]
    head_width = NOPE + ROPE
    heads = query.shape[1] // head_width
    scale = 1.0 / math.sqrt(head_width)
    pos = (block_ids[:, None] * qblock + jnp.arange(qblock, dtype=jnp.int32)[None, :]).reshape(-1)
    compressed, rope_keys = latent[:, :LATENT], latent[:, LATENT:]
    keys = jnp.dot(compressed, w_uk, preferred_element_type=F32).astype(BF16)
    values = jnp.dot(compressed, w_uv, preferred_element_type=F32).astype(BF16)

    def part(query_rows, query_pos):
        allowed = pos[None, :] <= query_pos[:, None]
        out = []
        for h in range(heads):
            q = query_rows[:, h * head_width : (h + 1) * head_width]
            k = keys[:, h * NOPE : (h + 1) * NOPE]
            scores = jnp.einsum("qd,kd->qk", q[:, :NOPE], k, preferred_element_type=F32)
            scores = scores + jnp.einsum(
                "qd,kd->qk", q[:, NOPE:], rope_keys, preferred_element_type=F32
            )
            scores = jnp.where(allowed, scores * scale, -1e30)
            top = jnp.max(scores, axis=1, keepdims=True)
            exponent = jnp.where(allowed, jnp.exp(scores - top), 0.0)
            total = jnp.sum(exponent, axis=1, keepdims=True)
            summed = jnp.dot(
                exponent.astype(BF16),
                values[:, h * NOPE : (h + 1) * NOPE],
                preferred_element_type=F32,
            )
            out.append((summed / total).astype(BF16))
        return jnp.concatenate(out, axis=1)

    tile = rows if rows <= 256 else 128
    if tile == rows:
        return part(query, pos)
    done = lax.map(
        lambda a: part(*a), (query.reshape(-1, tile, query.shape[1]), pos.reshape(-1, tile))
    )
    return done.reshape(rows, heads * NOPE)


def shards(
    latent,
    query,
    w_uk,
    w_uv,
    w_o,
    resid,
    norm_gain,
    w_gate,
    w_up,
    w_down,
    expert_ids,
    route_weights,
):
    ctx = lax.axis_size("ctx")
    groups = lax.axis_size(EH)
    me = lax.axis_index("ctx")
    mine = lax.axis_index(EH)
    qblock = query.shape[0]
    tok = resid.shape[0]
    cols = w_o.shape[1]
    width = resid.shape[1]
    ff = w_gate.shape[2]

    packed = jnp.concatenate([query, latent], axis=1)
    pieces = [packed] + [send(packed, "ctx", d) for d in range(1, ctx)]

    experts = jnp.arange(groups, dtype=jnp.int32)
    dense = jnp.sum(
        jnp.where(expert_ids[:, :, None] == experts, route_weights[:, :, None], 0.0), axis=1
    )
    resid_cols = resid.reshape(tok, ctx, cols).transpose(1, 0, 2)
    resid_parts, dense_parts = [], []
    for d in range(ctx):
        part = lax.dynamic_index_in_dim(resid_cols, (me + d) % ctx, 0, keepdims=False)
        resid_parts.append(send(part, "ctx", d) if d else part)
        dense_parts.append(send(dense, "ctx", d) if d else dense)

    gathered = jnp.concatenate(pieces, axis=0)
    block_ids = (me - jnp.arange(ctx, dtype=jnp.int32)) % ctx
    attended = attend(
        gathered[:, : query.shape[1]],
        gathered[:, query.shape[1] :],
        w_uk,
        w_uv,
        block_ids,
        qblock,
    )
    partial = jnp.dot(attended, w_o, preferred_element_type=F32).astype(BF16)
    partial = partial.reshape(ctx, groups, tok, cols)
    total = 0.0
    for s in range(groups):
        part = lax.dynamic_index_in_dim(partial, (mine + s) % groups, 1, keepdims=False)
        total = total + (send(part, EH, s) if s else part).astype(F32)
    total = total + jnp.stack(resid_parts).astype(F32)
    residual_sum = jnp.stack(ordered([total[d] for d in range(ctx)], me))
    dense_rows = jnp.concatenate(ordered(dense_parts, me), axis=0)

    travelling = residual_sum.astype(BF16).reshape(ctx * tok, cols)
    columns = [travelling] + [send(travelling, "ctx", d) for d in range(1, ctx)]
    rows = jnp.concatenate(ordered(columns, me), axis=1).astype(F32)
    inverse_rms = lax.rsqrt(jnp.mean(rows * rows, axis=1, keepdims=True) + 1e-06)
    normalized = (rows * inverse_rms * norm_gain).astype(BF16)
    everything = lax.all_gather(normalized, EH, axis=0, tiled=True)

    gate_part = jnp.dot(everything, w_gate[0], preferred_element_type=F32)
    up_part = jnp.dot(everything, w_up[0], preferred_element_type=F32)
    hidden = (jax.nn.silu(gate_part) * up_part).astype(BF16)
    hidden = [hidden] + [send(hidden, "ctx", d) for d in range(1, ctx)]
    hidden = jnp.concatenate(ordered(hidden, me), axis=1)
    expert_cols = jnp.dot(hidden, w_down[0], preferred_element_type=F32).astype(BF16)
    expert_cols = expert_cols.reshape(groups, ctx * tok, cols)
    moe = 0.0
    for s in range(groups):
        part = lax.dynamic_index_in_dim(expert_cols, (mine + s) % groups, 0, keepdims=False)
        part = (send(part, EH, s) if s else part).astype(F32)
        weight = lax.dynamic_slice_in_dim(dense_rows, (mine - s) % groups, 1, axis=1)
        moe = moe + part * weight
    final = (residual_sum.reshape(ctx * tok, cols) + moe).astype(BF16).reshape(ctx, tok, cols)
    out = []
    for d in range(ctx):
        part = lax.dynamic_index_in_dim(final, (me + d) % ctx, 0, keepdims=False)
        out.append(send(part, "ctx", d) if d else part)
    return jnp.concatenate(ordered(out, me), axis=1)


def lanes(ref, start, size):
    return ref[:, pl.ds(pl.multiple_of(start * size, 128), size)]


def call(kernel, out, args, flops, vmem):
    return pl.pallas_call(
        kernel,
        out_shape=out,
        in_specs=[pl.BlockSpec(memory_space=pltpu.VMEM)] * len(args),
        out_specs=jax.tree.map(lambda _: pl.BlockSpec(memory_space=pltpu.VMEM), out),
        compiler_params=pltpu.CompilerParams(vmem_limit_bytes=vmem << 20),
        cost_estimate=pl.CostEstimate(
            flops=flops, bytes_accessed=sum(a.size * a.dtype.itemsize for a in args),
            transcendentals=0,
        ),
    )(*args)


def wrap(value, size):
    return jnp.where(value < 0, value + size, jnp.where(value >= size, value - size, value))


def pack_kernel(ctx, groups, query, latent, resid, ids, weights, *outs):
    me = lax.axis_index("ctx")
    tok, cols = resid.shape[0], resid.shape[1] // ctx
    rows, width = query.shape
    parts = rows // tok
    lane = lax.broadcasted_iota(jnp.int32, (tok, 128), 1)
    high = jnp.zeros((tok, 128), F32)
    for k in range(ids.shape[1]):
        high = high + jnp.where(lane == ids[:, k : k + 1], weights[:, k : k + 1], 0.0)
    for k in range(ids.shape[1]):
        high = high + jnp.where(lane == ids[:, k : k + 1] + 64, weights[:, k : k + 1], 0.0)
    near = high.astype(BF16).astype(F32)
    routes = jnp.where(lane < 64, near, high - near)
    extra = (cols + 128) // parts
    for d, out in enumerate(outs):
        to = wrap(me + d, ctx)
        both = jnp.concatenate([lanes(resid, to, cols).astype(F32), routes], axis=1)
        both = jnp.concatenate([both[:, p * extra : (p + 1) * extra] for p in range(parts)], axis=0)
        out[:, :width] = query[...]
        out[:, width : width + extra] = both.astype(BF16)
        out[:, width + extra :] = latent[...]


def attention_kernel(ctx, groups, heads, extra, *refs):
    pieces, (w_uk, w_uv, w_o), outs, part_ref = (
        refs[:ctx],
        refs[ctx : ctx + 3],
        refs[ctx + 3 : -1],
        refs[-1],
    )
    me, mine = lax.axis_index("ctx"), lax.axis_index(EH)
    rows = pieces[0].shape[0]
    width = NOPE + ROPE
    scale = 1.0 / math.sqrt(width)
    first = heads * width + extra
    latent = jnp.concatenate([p[:, first : first + LATENT] for p in pieces], axis=0)
    rope_keys = jnp.concatenate([p[:, first + LATENT :] for p in pieces], axis=0)
    query = jnp.concatenate([p[:, : heads * width] for p in pieces], axis=0)
    keys = jnp.dot(latent, w_uk[...], preferred_element_type=F32).astype(BF16)
    values = jnp.dot(latent, w_uv[...], preferred_element_type=F32).astype(BF16)
    total = ctx * rows

    def place(dim):
        at = lax.broadcasted_iota(jnp.int32, (total, total), dim)
        block = jnp.zeros_like(at)
        for d in range(ctx):
            here = (at >= d * rows) & (at < (d + 1) * rows)
            block = jnp.where(here, wrap(me - d, ctx) * rows - d * rows, block)
        return at + block

    allowed = place(1) <= place(0)
    contract = (((1,), (1,)), ((), ()))
    done = []
    for h in range(heads):
        q = query[:, h * width : (h + 1) * width]
        k = jnp.concatenate([keys[:, h * NOPE : (h + 1) * NOPE], rope_keys], axis=1)
        scores = lax.dot_general(q, k, contract, preferred_element_type=F32) * scale
        scores = jnp.where(allowed, scores, -1e30)
        exponent = jnp.exp(scores - jnp.max(scores, axis=1, keepdims=True))
        exponent = jnp.where(allowed, exponent, 0.0)
        weight = jnp.sum(exponent, axis=1, keepdims=True)
        summed = jnp.dot(
            exponent.astype(BF16), values[:, h * NOPE : (h + 1) * NOPE], preferred_element_type=F32
        )
        done.append((summed / weight).astype(BF16))
    partial = jnp.dot(jnp.concatenate(done, axis=1), w_o[...], preferred_element_type=F32)
    tok = rows // groups
    for n in range(ctx * groups):
        part_ref[n] = partial[n * tok : (n + 1) * tok]
    for s, out in enumerate(outs):
        to = jnp.bitwise_xor(mine, s)
        out[...] = jnp.concatenate([part_ref[d * groups + to] for d in range(ctx)], axis=0).astype(
            BF16
        )


def residual_kernel(ctx, groups, first, extra, *refs):
    sums, pieces, (travelling, kept, routes) = refs[:groups], refs[groups : groups + ctx], refs[-3:]
    me = lax.axis_index("ctx")
    tok, cols = kept.shape[1:]
    total = sums[0][...].astype(F32)
    for part in sums[1:]:
        total = total + part[...].astype(F32)
    for d in range(ctx):
        both = pieces[d][:, first : first + extra].astype(F32)
        both = jnp.concatenate(
            [both[p * tok : (p + 1) * tok] for p in range(both.shape[0] // tok)], axis=1
        )
        at = wrap(me - d, ctx)
        kept[at] = total[d * tok : (d + 1) * tok] + both[:, :cols]
        routes[at] = both[:, cols:]
    travelling[...] = jnp.concatenate([kept[b] for b in range(ctx)], axis=0).astype(BF16)


def norm_kernel(ctx, *refs):
    columns, gain, out = refs[:ctx], refs[ctx], refs[ctx + 1]
    me = lax.axis_index("ctx")
    cols = columns[0].shape[1]
    values = [c[...].astype(F32) for c in columns]
    squares = values[0] * values[0]
    for v in values[1:]:
        squares = squares + v * v
    mean = jnp.sum(squares, axis=1, keepdims=True) * (1.0 / out.shape[1])
    inverse = lax.rsqrt(mean + 1e-06)
    for d, v in enumerate(values):
        at = pl.ds(pl.multiple_of(wrap(me - d, ctx) * cols, 128), cols)
        out[:, at] = (v * inverse * gain[:, at]).astype(BF16)


def hidden_kernel(near, far, w_gate, w_up, out):
    rows = jnp.concatenate([near[...], far[...]], axis=0)
    gate_part = jnp.dot(rows, w_gate[0], preferred_element_type=F32)
    up_part = jnp.dot(rows, w_up[0], preferred_element_type=F32)
    out[...] = (gate_part / (1.0 + jnp.exp(-gate_part)) * up_part).astype(BF16)


def down_kernel(ctx, *refs):
    hidden, w_down, outs = refs[:ctx], refs[ctx], refs[ctx + 1 :]
    me = lax.axis_index("ctx")
    ff = hidden[0].shape[1]
    total = 0.0
    for d in range(ctx):
        at = pl.ds(pl.multiple_of(wrap(me - d, ctx) * ff, ff), ff)
        total = total + jnp.dot(hidden[d][...], w_down[0, at, :], preferred_element_type=F32)
    rows = outs[0].shape[0]
    for n, out in enumerate(outs):
        out[...] = total[n * rows : (n + 1) * rows].astype(BF16)


def combine_kernel(ctx, groups, *refs):
    parts, kept, routes, outs = refs[:groups], refs[groups], refs[groups + 1], refs[groups + 2 : -1]
    final = refs[-1]
    me, mine = lax.axis_index("ctx"), lax.axis_index(EH)
    tok, cols = kept.shape[1:]
    weights = jnp.concatenate([routes[b] for b in range(ctx)], axis=0)
    total = jnp.concatenate([kept[b] for b in range(ctx)], axis=0)
    lane = lax.broadcasted_iota(jnp.int32, weights.shape, 1)
    for s, part in enumerate(parts):
        expert = jnp.bitwise_xor(mine, s)
        here = (lane == expert) | (lane == expert + 64)
        weight = jnp.sum(jnp.where(here, weights, 0.0), axis=1, keepdims=True)
        total = total + part[...].astype(F32) * weight
    for b in range(ctx):
        final[b] = total[b * tok : (b + 1) * tok]
    for d, out in enumerate(outs):
        out[...] = final[wrap(me + d, ctx)].astype(BF16)


def gather_kernel(ctx, *refs):
    parts, out = refs[:ctx], refs[ctx]
    me = lax.axis_index("ctx")
    cols = parts[0].shape[1]
    for d, part in enumerate(parts):
        out[:, pl.ds(pl.multiple_of(wrap(me - d, ctx) * cols, 128), cols)] = part[...]


def swap(value, step):
    size = lax.axis_size(EH)
    return lax.ppermute(value, EH, [(i, i ^ step) for i in range(size)])


def around(value, ctx):
    return [value] + [send(value, "ctx", d) for d in range(1, ctx)]


def fast_shards(
    latent, query, w_uk, w_uv, w_o, resid, norm_gain, w_gate, w_up, w_down, expert_ids, route_weights
):
    ctx, groups = lax.axis_size("ctx"), lax.axis_size(EH)
    rows, width = query.shape
    heads = width // (NOPE + ROPE)
    tok, model = resid.shape
    cols = w_o.shape[1]
    ff = w_gate.shape[2]
    extra = (cols + 128) * tok // rows
    here = ctx * tok
    like = jax.ShapeDtypeStruct

    packed = like((rows, width + extra + latent.shape[1]), BF16)
    packs = call(
        functools.partial(pack_kernel, ctx, groups),
        [packed] * ctx,
        [query, latent, resid, expert_ids, route_weights],
        0,
        8,
    )
    pieces = [packs[0]] + [send(packs[d], "ctx", d) for d in range(1, ctx)]
    partial = pl.pallas_call(
        functools.partial(attention_kernel, ctx, groups, heads, extra),
        out_shape=[like((here, cols), BF16)] * groups,
        in_specs=[pl.BlockSpec(memory_space=pltpu.VMEM)] * (ctx + 3),
        out_specs=[pl.BlockSpec(memory_space=pltpu.VMEM)] * groups,
        scratch_shapes=[pltpu.VMEM((ctx * groups, tok, cols), F32)],
        compiler_params=pltpu.CompilerParams(vmem_limit_bytes=16 << 20),
        cost_estimate=pl.CostEstimate(
            flops=2 * ctx * rows * heads * NOPE * (2 * LATENT + cols),
            bytes_accessed=4 << 20,
            transcendentals=heads * (ctx * rows) ** 2,
        ),
    )(*pieces, w_uk, w_uv, w_o)
    sums = [partial[0]] + [swap(partial[s], s) for s in range(1, groups)]
    travelling, kept, routes = call(
        functools.partial(residual_kernel, ctx, groups, width, extra),
        [like((here, cols), BF16), like((ctx, tok, cols), F32), like((ctx, tok, 128), F32)],
        sums + pieces,
        0,
        8,
    )
    mine = call(
        functools.partial(norm_kernel, ctx),
        like((here, model), BF16),
        around(travelling, ctx) + [norm_gain.reshape(1, model)],
        0,
        8,
    )
    work = 4 * 2 * here * model * ff
    sibling, other = swap(mine, 1), swap(mine, groups // 2)
    hidden = call(
        hidden_kernel, like((2 * here, ff), BF16), [mine, sibling, w_gate, w_up], work, 16
    )
    near = around(hidden, ctx)
    other_sibling = swap(other, 1)
    hidden = call(
        hidden_kernel, like((2 * here, ff), BF16), [other, other_sibling, w_gate, w_up], work, 16
    )
    far = around(hidden, ctx)
    down = functools.partial(down_kernel, ctx)
    pair = [like((here, cols), BF16)] * 2
    near = call(down, pair, near + [w_down], work // 2, 16)
    far = call(down, pair, far + [w_down], work // 2, 16)
    parts = [near[0], swap(near[1], 1), swap(far[0], groups // 2), swap(far[1], groups // 2 + 1)]
    finals = pl.pallas_call(
        functools.partial(combine_kernel, ctx, groups),
        out_shape=[like((tok, cols), BF16)] * ctx,
        in_specs=[pl.BlockSpec(memory_space=pltpu.VMEM)] * (groups + 2),
        out_specs=[pl.BlockSpec(memory_space=pltpu.VMEM)] * ctx,
        scratch_shapes=[pltpu.VMEM((ctx, tok, cols), F32)],
        compiler_params=pltpu.CompilerParams(vmem_limit_bytes=8 << 20),
    )(*parts, kept, routes)
    return call(
        functools.partial(gather_kernel, ctx),
        like((tok, model), BF16),
        [finals[0]] + [send(finals[d], "ctx", d) for d in range(1, ctx)],
        0,
        8,
    )


def solution(mesh):
    placed = (
        P(("groups", "ctx"), None),
        P(("groups", "ctx"), ("exp", "head")),
        P(None, ("exp", "head")),
        P(None, ("exp", "head")),
        P(("exp", "head"), "ctx"),
        P(("groups", "ctx", "exp", "head"), None),
        P(),
        P(("exp", "head"), None, "ctx"),
        P(("exp", "head"), None, "ctx"),
        P(("exp", "head"), None, "ctx"),
        P(("groups", "ctx", "exp", "head"), None),
        P(("groups", "ctx", "exp", "head"), None),
    )
    experts = mesh.shape["exp"] * mesh.shape["head"]

    def step(*args):
        cols, rows = args[4].shape[1], args[1].shape[0]
        parts = rows // args[5].shape[0]
        whole = cols % 128 == 0 and (cols + 128) % (128 * parts) == 0 and parts == experts
        small = rows * mesh.shape["ctx"] <= 256
        return (fast_shards if experts == 4 and whole and small else shards)(*args)

    return jax.shard_map(
        step,
        mesh=mesh,
        in_specs=placed,
        out_specs=P(("groups", "ctx", "exp", "head"), None),
        check_vma=False,
    )
```

```python
import functools
import math

import jax
import jax.numpy as jnp
from jax import lax
from jax.experimental import pallas as pl
from jax.experimental.pallas import tpu as pltpu
from jax.sharding import PartitionSpec as P

NOPE = 128
ROPE = 64
LATENT = 512
EH = ("exp", "head")
F32 = jnp.float32
BF16 = jnp.bfloat16


def send(value, axis, step):
    size = lax.axis_size(axis)
    return lax.ppermute(value, axis, [(i, (i + step) % size) for i in range(size)])


def ordered(pieces, me):
    size = len(pieces)
    stacked = jnp.stack(pieces)
    return [
        lax.dynamic_index_in_dim(stacked, (me - b) % size, 0, keepdims=False) for b in range(size)
    ]


def attend(query, latent, w_uk, w_uv, block_ids, qblock):
    rows = query.shape[0]
    head_width = NOPE + ROPE
    heads = query.shape[1] // head_width
    scale = 1.0 / math.sqrt(head_width)
    pos = (block_ids[:, None] * qblock + jnp.arange(qblock, dtype=jnp.int32)[None, :]).reshape(-1)
    compressed, rope_keys = latent[:, :LATENT], latent[:, LATENT:]
    keys = jnp.dot(compressed, w_uk, preferred_element_type=F32).astype(BF16)
    values = jnp.dot(compressed, w_uv, preferred_element_type=F32).astype(BF16)

    def part(query_rows, query_pos):
        allowed = pos[None, :] <= query_pos[:, None]
        out = []
        for h in range(heads):
            q = query_rows[:, h * head_width : (h + 1) * head_width]
            k = keys[:, h * NOPE : (h + 1) * NOPE]
            scores = jnp.einsum("qd,kd->qk", q[:, :NOPE], k, preferred_element_type=F32)
            scores = scores + jnp.einsum(
                "qd,kd->qk", q[:, NOPE:], rope_keys, preferred_element_type=F32
            )
            scores = jnp.where(allowed, scores * scale, -1e30)
            top = jnp.max(scores, axis=1, keepdims=True)
            exponent = jnp.where(allowed, jnp.exp(scores - top), 0.0)
            total = jnp.sum(exponent, axis=1, keepdims=True)
            summed = jnp.dot(
                exponent.astype(BF16),
                values[:, h * NOPE : (h + 1) * NOPE],
                preferred_element_type=F32,
            )
            out.append((summed / total).astype(BF16))
        return jnp.concatenate(out, axis=1)

    tile = rows if rows <= 256 else 128
    if tile == rows:
        return part(query, pos)
    done = lax.map(
        lambda a: part(*a), (query.reshape(-1, tile, query.shape[1]), pos.reshape(-1, tile))
    )
    return done.reshape(rows, heads * NOPE)


def shards(
    latent,
    query,
    w_uk,
    w_uv,
    w_o,
    resid,
    norm_gain,
    w_gate,
    w_up,
    w_down,
    expert_ids,
    route_weights,
):
    ctx = lax.axis_size("ctx")
    groups = lax.axis_size(EH)
    me = lax.axis_index("ctx")
    mine = lax.axis_index(EH)
    qblock = query.shape[0]
    tok = resid.shape[0]
    cols = w_o.shape[1]
    width = resid.shape[1]
    ff = w_gate.shape[2]

    packed = jnp.concatenate([query, latent], axis=1)
    pieces = [packed] + [send(packed, "ctx", d) for d in range(1, ctx)]

    experts = jnp.arange(groups, dtype=jnp.int32)
    dense = jnp.sum(
        jnp.where(expert_ids[:, :, None] == experts, route_weights[:, :, None], 0.0), axis=1
    )
    resid_cols = resid.reshape(tok, ctx, cols).transpose(1, 0, 2)
    resid_parts, dense_parts = [], []
    for d in range(ctx):
        part = lax.dynamic_index_in_dim(resid_cols, (me + d) % ctx, 0, keepdims=False)
        resid_parts.append(send(part, "ctx", d) if d else part)
        dense_parts.append(send(dense, "ctx", d) if d else dense)

    gathered = jnp.concatenate(pieces, axis=0)
    block_ids = (me - jnp.arange(ctx, dtype=jnp.int32)) % ctx
    attended = attend(
        gathered[:, : query.shape[1]],
        gathered[:, query.shape[1] :],
        w_uk,
        w_uv,
        block_ids,
        qblock,
    )
    partial = jnp.dot(attended, w_o, preferred_element_type=F32).astype(BF16)
    partial = partial.reshape(ctx, groups, tok, cols)
    total = 0.0
    for s in range(groups):
        part = lax.dynamic_index_in_dim(partial, (mine + s) % groups, 1, keepdims=False)
        total = total + (send(part, EH, s) if s else part).astype(F32)
    total = total + jnp.stack(resid_parts).astype(F32)
    residual_sum = jnp.stack(ordered([total[d] for d in range(ctx)], me))
    dense_rows = jnp.concatenate(ordered(dense_parts, me), axis=0)

    travelling = residual_sum.astype(BF16).reshape(ctx * tok, cols)
    columns = [travelling] + [send(travelling, "ctx", d) for d in range(1, ctx)]
    rows = jnp.concatenate(ordered(columns, me), axis=1).astype(F32)
    inverse_rms = lax.rsqrt(jnp.mean(rows * rows, axis=1, keepdims=True) + 1e-06)
    normalized = (rows * inverse_rms * norm_gain).astype(BF16)
    everything = lax.all_gather(normalized, EH, axis=0, tiled=True)

    gate_part = jnp.dot(everything, w_gate[0], preferred_element_type=F32)
    up_part = jnp.dot(everything, w_up[0], preferred_element_type=F32)
    hidden = (jax.nn.silu(gate_part) * up_part).astype(BF16)
    hidden = [hidden] + [send(hidden, "ctx", d) for d in range(1, ctx)]
    hidden = jnp.concatenate(ordered(hidden, me), axis=1)
    expert_cols = jnp.dot(hidden, w_down[0], preferred_element_type=F32).astype(BF16)
    expert_cols = expert_cols.reshape(groups, ctx * tok, cols)
    moe = 0.0
    for s in range(groups):
        part = lax.dynamic_index_in_dim(expert_cols, (mine + s) % groups, 0, keepdims=False)
        part = (send(part, EH, s) if s else part).astype(F32)
        weight = lax.dynamic_slice_in_dim(dense_rows, (mine - s) % groups, 1, axis=1)
        moe = moe + part * weight
    final = (residual_sum.reshape(ctx * tok, cols) + moe).astype(BF16).reshape(ctx, tok, cols)
    out = []
    for d in range(ctx):
        part = lax.dynamic_index_in_dim(final, (me + d) % ctx, 0, keepdims=False)
        out.append(send(part, "ctx", d) if d else part)
    return jnp.concatenate(ordered(out, me), axis=1)


def lanes(ref, start, size):
    return ref[:, pl.ds(pl.multiple_of(start * size, 128), size)]


def call(kernel, out, args, flops, vmem):
    return pl.pallas_call(
        kernel,
        out_shape=out,
        in_specs=[pl.BlockSpec(memory_space=pltpu.VMEM)] * len(args),
        out_specs=jax.tree.map(lambda _: pl.BlockSpec(memory_space=pltpu.VMEM), out),
        compiler_params=pltpu.CompilerParams(vmem_limit_bytes=vmem << 20),
        cost_estimate=pl.CostEstimate(
            flops=flops, bytes_accessed=sum(a.size * a.dtype.itemsize for a in args),
            transcendentals=0,
        ),
    )(*args)


def wrap(value, size):
    return jnp.where(value < 0, value + size, jnp.where(value >= size, value - size, value))


def pack_kernel(ctx, groups, *refs):
    query, latent, resid, ids, weights = refs[:5]
    outs = refs[6:]
    me = lax.axis_index("ctx")
    tok, cols = resid.shape[0], resid.shape[1] // ctx
    rows, width = query.shape
    parts = rows // tok
    lane = lax.broadcasted_iota(jnp.int32, (tok, 128), 1)
    same = lax.broadcasted_iota(jnp.int32, (tok, tok), 0) == lax.broadcasted_iota(
        jnp.int32, (tok, tok), 1
    )
    full = jnp.zeros((tok, 128), F32)
    for k in range(ids.shape[0]):
        expert = jnp.sum(jnp.where(same, ids[k : k + 1, :], 0), axis=1, keepdims=True)
        weight = jnp.sum(jnp.where(same, weights[k : k + 1, :], 0.0), axis=1, keepdims=True)
        full = full + jnp.where((lane == expert) | (lane == expert + 64), weight, 0.0)
    near = full.astype(BF16).astype(F32)
    routes = jnp.where(lane < 64, near, full - near)
    extra = (cols + 128) // parts
    for d, out in enumerate(outs):
        to = wrap(me + d, ctx)
        both = jnp.concatenate([lanes(resid, to, cols).astype(F32), routes], axis=1)
        both = jnp.concatenate([both[:, p * extra : (p + 1) * extra] for p in range(parts)], axis=0)
        out[:, :width] = query[...]
        out[:, width : width + extra] = both.astype(BF16)
        out[:, width + extra :] = latent[...]


def open_kernel(out):
    out[...] = jnp.zeros_like(out)


def hold_kernel(value, after, out):
    out[:16, :128] = value[:16, :128]


def hold(value, after):
    return pl.pallas_call(
        hold_kernel,
        out_shape=jax.ShapeDtypeStruct(value.shape, value.dtype),
        in_specs=[
            pl.BlockSpec(memory_space=pltpu.VMEM),
            pl.BlockSpec(memory_space=pl.ANY),
        ],
        out_specs=pl.BlockSpec(memory_space=pltpu.VMEM),
        input_output_aliases={0: 0},
        compiler_params=pltpu.CompilerParams(vmem_limit_bytes=4 << 20),
    )(value, after)


def attention_kernel(ctx, groups, heads, extra, *refs):
    pieces, (w_uk, w_uv, w_o), outs, part_ref = (
        refs[:ctx],
        refs[ctx : ctx + 3],
        refs[ctx + 3 : -1],
        refs[-1],
    )
    me, mine = lax.axis_index("ctx"), lax.axis_index(EH)
    rows = pieces[0].shape[0]
    width = NOPE + ROPE
    scale = 1.0 / math.sqrt(width)
    first = heads * width + extra
    latent = jnp.concatenate([p[:, first : first + LATENT] for p in pieces], axis=0)
    rope_keys = jnp.concatenate([p[:, first + LATENT :] for p in pieces], axis=0)
    query = jnp.concatenate([p[:, : heads * width] for p in pieces], axis=0)
    keys = jnp.dot(latent, w_uk[...], preferred_element_type=F32).astype(BF16)
    values = jnp.dot(latent, w_uv[...], preferred_element_type=F32).astype(BF16)
    total = ctx * rows

    def place(dim):
        at = lax.broadcasted_iota(jnp.int32, (total, total), dim)
        block = jnp.zeros_like(at)
        for d in range(ctx):
            here = (at >= d * rows) & (at < (d + 1) * rows)
            block = jnp.where(here, wrap(me - d, ctx) * rows - d * rows, block)
        return at + block

    allowed = place(1) <= place(0)
    contract = (((1,), (1,)), ((), ()))
    done = []
    for h in range(heads):
        q = query[:, h * width : (h + 1) * width]
        k = jnp.concatenate([keys[:, h * NOPE : (h + 1) * NOPE], rope_keys], axis=1)
        scores = lax.dot_general(q, k, contract, preferred_element_type=F32) * scale
        scores = jnp.where(allowed, scores, -1e30)
        exponent = jnp.exp(scores - jnp.max(scores, axis=1, keepdims=True))
        exponent = jnp.where(allowed, exponent, 0.0)
        weight = jnp.sum(exponent, axis=1, keepdims=True)
        summed = jnp.dot(
            exponent.astype(BF16), values[:, h * NOPE : (h + 1) * NOPE], preferred_element_type=F32
        )
        done.append((summed / weight).astype(BF16))
    partial = jnp.dot(jnp.concatenate(done, axis=1), w_o[...], preferred_element_type=F32)
    tok = rows // groups
    for n in range(ctx * groups):
        part_ref[n] = partial[n * tok : (n + 1) * tok]
    for s, out in enumerate(outs):
        to = jnp.bitwise_xor(mine, s)
        out[...] = jnp.concatenate([part_ref[d * groups + to] for d in range(ctx)], axis=0).astype(
            BF16
        )


def residual_kernel(ctx, groups, first, extra, *refs):
    sums, pieces, (travelling, kept, routes) = refs[:groups], refs[groups : groups + ctx], refs[-3:]
    me = lax.axis_index("ctx")
    tok, cols = kept.shape[1:]
    total = sums[0][...].astype(F32)
    for part in sums[1:]:
        total = total + part[...].astype(F32)
    for d in range(ctx):
        both = pieces[d][:, first : first + extra].astype(F32)
        both = jnp.concatenate(
            [both[p * tok : (p + 1) * tok] for p in range(both.shape[0] // tok)], axis=1
        )
        at = wrap(me - d, ctx)
        kept[at] = total[d * tok : (d + 1) * tok] + both[:, :cols]
        routes[at] = both[:, cols:]
    travelling[...] = jnp.concatenate([kept[b] for b in range(ctx)], axis=0).astype(BF16)


def norm_kernel(ctx, *refs):
    columns, gain, out = refs[:ctx], refs[ctx], refs[ctx + 1]
    me = lax.axis_index("ctx")
    cols = columns[0].shape[1]
    values = [c[...].astype(F32) for c in columns]
    squares = values[0] * values[0]
    for v in values[1:]:
        squares = squares + v * v
    mean = jnp.sum(squares, axis=1, keepdims=True) * (1.0 / out.shape[1])
    inverse = lax.rsqrt(mean + 1e-06)
    for d, v in enumerate(values):
        at = pl.ds(pl.multiple_of(wrap(me - d, ctx) * cols, 128), cols)
        out[:, at] = (v * inverse * gain[:, at]).astype(BF16)


def hidden_kernel(near, far, w_gate, w_up, out):
    rows = jnp.concatenate([near[...], far[...]], axis=0)
    gate_part = jnp.dot(rows, w_gate[0], preferred_element_type=F32)
    up_part = jnp.dot(rows, w_up[0], preferred_element_type=F32)
    out[...] = (gate_part / (1.0 + jnp.exp(-gate_part)) * up_part).astype(BF16)


def down_kernel(ctx, *refs):
    hidden, w_down, outs = refs[:ctx], refs[ctx], refs[ctx + 1 :]
    me = lax.axis_index("ctx")
    ff = hidden[0].shape[1]
    total = 0.0
    for d in range(ctx):
        at = pl.ds(pl.multiple_of(wrap(me - d, ctx) * ff, ff), ff)
        total = total + jnp.dot(hidden[d][...], w_down[0, at, :], preferred_element_type=F32)
    rows = outs[0].shape[0]
    for n, out in enumerate(outs):
        out[...] = total[n * rows : (n + 1) * rows].astype(BF16)


def combine_kernel(ctx, groups, *refs):
    parts, kept, routes, outs = refs[:groups], refs[groups], refs[groups + 1], refs[groups + 2 : -1]
    final = refs[-1]
    me, mine = lax.axis_index("ctx"), lax.axis_index(EH)
    tok, cols = kept.shape[1:]
    weights = jnp.concatenate([routes[b] for b in range(ctx)], axis=0)
    total = jnp.concatenate([kept[b] for b in range(ctx)], axis=0)
    lane = lax.broadcasted_iota(jnp.int32, weights.shape, 1)
    for s, part in enumerate(parts):
        expert = jnp.bitwise_xor(mine, s)
        here = (lane == expert) | (lane == expert + 64)
        weight = jnp.sum(jnp.where(here, weights, 0.0), axis=1, keepdims=True)
        total = total + part[...].astype(F32) * weight
    for b in range(ctx):
        final[b] = total[b * tok : (b + 1) * tok]
    for d, out in enumerate(outs):
        out[...] = final[wrap(me + d, ctx)].astype(BF16)


def gather_kernel(ctx, *refs):
    parts, out = refs[:ctx], refs[ctx]
    me = lax.axis_index("ctx")
    cols = parts[0].shape[1]
    for d, part in enumerate(parts):
        out[:, pl.ds(pl.multiple_of(wrap(me - d, ctx) * cols, 128), cols)] = part[...]


def swap(value, step):
    size = lax.axis_size(EH)
    return lax.ppermute(value, EH, [(i, i ^ step) for i in range(size)])


def around(value, ctx):
    return [value] + [send(value, "ctx", d) for d in range(1, ctx)]


def fast_shards(
    latent, query, w_uk, w_uv, w_o, resid, norm_gain, w_gate, w_up, w_down, expert_ids, route_weights
):
    ctx, groups = lax.axis_size("ctx"), lax.axis_size(EH)
    rows, width = query.shape
    heads = width // (NOPE + ROPE)
    tok, model = resid.shape
    cols = w_o.shape[1]
    ff = w_gate.shape[2]
    extra = (cols + 128) * tok // rows
    here = ctx * tok
    like = jax.ShapeDtypeStruct

    packed = like((rows, width + extra + latent.shape[1]), BF16)
    sources = [query, latent, resid, expert_ids.T, route_weights.T]
    opened = pl.pallas_call(
        open_kernel,
        out_shape=like((8, 128), F32),
        compiler_params=pltpu.CompilerParams(vmem_limit_bytes=1 << 20),
        cost_estimate=pl.CostEstimate(flops=1 << 31, bytes_accessed=0, transcendentals=0),
    )()
    packs = call(
        functools.partial(pack_kernel, ctx, groups),
        [packed] * ctx,
        sources + [opened],
        1 << 32,
        8,
    )
    pieces = [packs[0]] + [send(packs[d], "ctx", d) for d in range(1, ctx)]
    partial = pl.pallas_call(
        functools.partial(attention_kernel, ctx, groups, heads, extra),
        out_shape=[like((here, cols), BF16)] * groups,
        in_specs=[pl.BlockSpec(memory_space=pltpu.VMEM)] * (ctx + 3),
        out_specs=[pl.BlockSpec(memory_space=pltpu.VMEM)] * groups,
        scratch_shapes=[pltpu.VMEM((ctx * groups, tok, cols), F32)],
        compiler_params=pltpu.CompilerParams(vmem_limit_bytes=16 << 20),
        cost_estimate=pl.CostEstimate(
            flops=2 * ctx * rows * heads * NOPE * (2 * LATENT + cols),
            bytes_accessed=4 << 20,
            transcendentals=heads * (ctx * rows) ** 2,
        ),
    )(*pieces, w_uk, w_uv, w_o)
    sums = [partial[0]] + [swap(partial[s], s) for s in range(1, groups)]
    travelling, kept, routes = call(
        functools.partial(residual_kernel, ctx, groups, width, extra),
        [like((here, cols), BF16), like((ctx, tok, cols), F32), like((ctx, tok, 128), F32)],
        sums + pieces,
        0,
        8,
    )
    mine = call(
        functools.partial(norm_kernel, ctx),
        like((here, model), BF16),
        around(travelling, ctx) + [norm_gain.reshape(1, model)],
        0,
        8,
    )
    work = 4 * 2 * here * model * ff
    sibling, other = swap(mine, 1), swap(mine, groups // 2)
    hidden = call(
        hidden_kernel, like((2 * here, ff), BF16), [mine, sibling, w_gate, w_up], work, 16
    )
    near = around(hidden, ctx)
    other = hold(other, hidden)
    other_sibling = swap(other, 1)
    hidden = call(
        hidden_kernel, like((2 * here, ff), BF16), [other, other_sibling, w_gate, w_up], work, 16
    )
    far = around(hidden, ctx)
    down = functools.partial(down_kernel, ctx)
    pair = [like((here, cols), BF16)] * 2
    near = call(down, pair, near + [w_down], work // 2, 16)
    far = call(down, pair, far + [w_down], work // 2, 16)
    parts = [near[0], swap(near[1], 1), swap(far[0], groups // 2), swap(far[1], groups // 2 + 1)]
    finals = pl.pallas_call(
        functools.partial(combine_kernel, ctx, groups),
        out_shape=[like((tok, cols), BF16)] * ctx,
        in_specs=[pl.BlockSpec(memory_space=pltpu.VMEM)] * (groups + 2),
        out_specs=[pl.BlockSpec(memory_space=pltpu.VMEM)] * ctx,
        scratch_shapes=[pltpu.VMEM((ctx, tok, cols), F32)],
        compiler_params=pltpu.CompilerParams(vmem_limit_bytes=8 << 20),
    )(*parts, kept, routes)
    return call(
        functools.partial(gather_kernel, ctx),
        like((tok, model), BF16),
        [finals[0]] + [send(finals[d], "ctx", d) for d in range(1, ctx)],
        0,
        8,
    )


def solution(mesh):
    placed = (
        P(("groups", "ctx"), None),
        P(("groups", "ctx"), ("exp", "head")),
        P(None, ("exp", "head")),
        P(None, ("exp", "head")),
        P(("exp", "head"), "ctx"),
        P(("groups", "ctx", "exp", "head"), None),
        P(),
        P(("exp", "head"), None, "ctx"),
        P(("exp", "head"), None, "ctx"),
        P(("exp", "head"), None, "ctx"),
        P(("groups", "ctx", "exp", "head"), None),
        P(("groups", "ctx", "exp", "head"), None),
    )
    experts = mesh.shape["exp"] * mesh.shape["head"]

    def step(*args):
        cols, rows = args[4].shape[1], args[1].shape[0]
        parts = rows // args[5].shape[0]
        whole = cols % 128 == 0 and (cols + 128) % (128 * parts) == 0 and parts == experts
        small = rows * mesh.shape["ctx"] <= 256
        return (fast_shards if experts == 4 and whole and small else shards)(*args)

    return jax.shard_map(
        step,
        mesh=mesh,
        in_specs=placed,
        out_specs=P(("groups", "ctx", "exp", "head"), None),
        check_vma=False,
    )
```

```python
import functools
import math

import jax
import jax.numpy as jnp
from jax import lax
from jax.experimental import pallas as pl
from jax.experimental.pallas import tpu as pltpu
from jax.sharding import PartitionSpec as P

NOPE = 128
ROPE = 64
LATENT = 512
EH = ("exp", "head")
F32 = jnp.float32
BF16 = jnp.bfloat16


def send(value, axis, step):
    size = lax.axis_size(axis)
    return lax.ppermute(value, axis, [(i, (i + step) % size) for i in range(size)])


def ordered(pieces, me):
    size = len(pieces)
    stacked = jnp.stack(pieces)
    return [
        lax.dynamic_index_in_dim(stacked, (me - b) % size, 0, keepdims=False) for b in range(size)
    ]


def attend(query, latent, w_uk, w_uv, block_ids, qblock):
    rows = query.shape[0]
    head_width = NOPE + ROPE
    heads = query.shape[1] // head_width
    scale = 1.0 / math.sqrt(head_width)
    pos = (block_ids[:, None] * qblock + jnp.arange(qblock, dtype=jnp.int32)[None, :]).reshape(-1)
    compressed, rope_keys = latent[:, :LATENT], latent[:, LATENT:]
    keys = jnp.dot(compressed, w_uk, preferred_element_type=F32).astype(BF16)
    values = jnp.dot(compressed, w_uv, preferred_element_type=F32).astype(BF16)

    def part(query_rows, query_pos):
        allowed = pos[None, :] <= query_pos[:, None]
        out = []
        for h in range(heads):
            q = query_rows[:, h * head_width : (h + 1) * head_width]
            k = keys[:, h * NOPE : (h + 1) * NOPE]
            scores = jnp.einsum("qd,kd->qk", q[:, :NOPE], k, preferred_element_type=F32)
            scores = scores + jnp.einsum(
                "qd,kd->qk", q[:, NOPE:], rope_keys, preferred_element_type=F32
            )
            scores = jnp.where(allowed, scores * scale, -1e30)
            top = jnp.max(scores, axis=1, keepdims=True)
            exponent = jnp.where(allowed, jnp.exp(scores - top), 0.0)
            total = jnp.sum(exponent, axis=1, keepdims=True)
            summed = jnp.dot(
                exponent.astype(BF16),
                values[:, h * NOPE : (h + 1) * NOPE],
                preferred_element_type=F32,
            )
            out.append((summed / total).astype(BF16))
        return jnp.concatenate(out, axis=1)

    tile = rows if rows <= 256 else 128
    if tile == rows:
        return part(query, pos)
    done = lax.map(
        lambda a: part(*a), (query.reshape(-1, tile, query.shape[1]), pos.reshape(-1, tile))
    )
    return done.reshape(rows, heads * NOPE)


def shards(
    latent,
    query,
    w_uk,
    w_uv,
    w_o,
    resid,
    norm_gain,
    w_gate,
    w_up,
    w_down,
    expert_ids,
    route_weights,
):
    ctx = lax.axis_size("ctx")
    groups = lax.axis_size(EH)
    me = lax.axis_index("ctx")
    mine = lax.axis_index(EH)
    qblock = query.shape[0]
    tok = resid.shape[0]
    cols = w_o.shape[1]
    width = resid.shape[1]
    ff = w_gate.shape[2]

    packed = jnp.concatenate([query, latent], axis=1)
    pieces = [packed] + [send(packed, "ctx", d) for d in range(1, ctx)]

    experts = jnp.arange(groups, dtype=jnp.int32)
    dense = jnp.sum(
        jnp.where(expert_ids[:, :, None] == experts, route_weights[:, :, None], 0.0), axis=1
    )
    resid_cols = resid.reshape(tok, ctx, cols).transpose(1, 0, 2)
    resid_parts, dense_parts = [], []
    for d in range(ctx):
        part = lax.dynamic_index_in_dim(resid_cols, (me + d) % ctx, 0, keepdims=False)
        resid_parts.append(send(part, "ctx", d) if d else part)
        dense_parts.append(send(dense, "ctx", d) if d else dense)

    gathered = jnp.concatenate(pieces, axis=0)
    block_ids = (me - jnp.arange(ctx, dtype=jnp.int32)) % ctx
    attended = attend(
        gathered[:, : query.shape[1]],
        gathered[:, query.shape[1] :],
        w_uk,
        w_uv,
        block_ids,
        qblock,
    )
    partial = jnp.dot(attended, w_o, preferred_element_type=F32).astype(BF16)
    partial = partial.reshape(ctx, groups, tok, cols)
    total = 0.0
    for s in range(groups):
        part = lax.dynamic_index_in_dim(partial, (mine + s) % groups, 1, keepdims=False)
        total = total + (send(part, EH, s) if s else part).astype(F32)
    total = total + jnp.stack(resid_parts).astype(F32)
    residual_sum = jnp.stack(ordered([total[d] for d in range(ctx)], me))
    dense_rows = jnp.concatenate(ordered(dense_parts, me), axis=0)

    travelling = residual_sum.astype(BF16).reshape(ctx * tok, cols)
    columns = [travelling] + [send(travelling, "ctx", d) for d in range(1, ctx)]
    rows = jnp.concatenate(ordered(columns, me), axis=1).astype(F32)
    inverse_rms = lax.rsqrt(jnp.mean(rows * rows, axis=1, keepdims=True) + 1e-06)
    normalized = (rows * inverse_rms * norm_gain).astype(BF16)
    everything = lax.all_gather(normalized, EH, axis=0, tiled=True)

    gate_part = jnp.dot(everything, w_gate[0], preferred_element_type=F32)
    up_part = jnp.dot(everything, w_up[0], preferred_element_type=F32)
    hidden = (jax.nn.silu(gate_part) * up_part).astype(BF16)
    hidden = [hidden] + [send(hidden, "ctx", d) for d in range(1, ctx)]
    hidden = jnp.concatenate(ordered(hidden, me), axis=1)
    expert_cols = jnp.dot(hidden, w_down[0], preferred_element_type=F32).astype(BF16)
    expert_cols = expert_cols.reshape(groups, ctx * tok, cols)
    moe = 0.0
    for s in range(groups):
        part = lax.dynamic_index_in_dim(expert_cols, (mine + s) % groups, 0, keepdims=False)
        part = (send(part, EH, s) if s else part).astype(F32)
        weight = lax.dynamic_slice_in_dim(dense_rows, (mine - s) % groups, 1, axis=1)
        moe = moe + part * weight
    final = (residual_sum.reshape(ctx * tok, cols) + moe).astype(BF16).reshape(ctx, tok, cols)
    out = []
    for d in range(ctx):
        part = lax.dynamic_index_in_dim(final, (me + d) % ctx, 0, keepdims=False)
        out.append(send(part, "ctx", d) if d else part)
    return jnp.concatenate(ordered(out, me), axis=1)


def lanes(ref, start, size):
    return ref[:, pl.ds(pl.multiple_of(start * size, 128), size)]


def call(kernel, out, args, flops, vmem):
    return pl.pallas_call(
        kernel,
        out_shape=out,
        in_specs=[pl.BlockSpec(memory_space=pltpu.VMEM)] * len(args),
        out_specs=jax.tree.map(lambda _: pl.BlockSpec(memory_space=pltpu.VMEM), out),
        compiler_params=pltpu.CompilerParams(vmem_limit_bytes=vmem << 20),
        cost_estimate=pl.CostEstimate(
            flops=flops, bytes_accessed=sum(a.size * a.dtype.itemsize for a in args),
            transcendentals=0,
        ),
    )(*args)


def wrap(value, size):
    return jnp.where(value < 0, value + size, jnp.where(value >= size, value - size, value))


def pack_kernel(ctx, groups, *refs):
    query, latent, resid, ids, weights = refs[:5]
    outs = refs[6:]
    me = lax.axis_index("ctx")
    tok, cols = resid.shape[0], resid.shape[1] // ctx
    rows, width = query.shape
    parts = rows // tok
    lane = lax.broadcasted_iota(jnp.int32, (tok, 128), 1)
    same = lax.broadcasted_iota(jnp.int32, (tok, tok), 0) == lax.broadcasted_iota(
        jnp.int32, (tok, tok), 1
    )
    full = jnp.zeros((tok, 128), F32)
    for k in range(ids.shape[0]):
        expert = jnp.sum(jnp.where(same, ids[k : k + 1, :], 0), axis=1, keepdims=True)
        weight = jnp.sum(jnp.where(same, weights[k : k + 1, :], 0.0), axis=1, keepdims=True)
        full = full + jnp.where((lane == expert) | (lane == expert + 64), weight, 0.0)
    near = full.astype(BF16).astype(F32)
    routes = jnp.where(lane < 64, near, full - near)
    extra = (cols + 128) // parts
    for d, out in enumerate(outs):
        to = wrap(me + d, ctx)
        both = jnp.concatenate([lanes(resid, to, cols).astype(F32), routes], axis=1)
        both = jnp.concatenate([both[:, p * extra : (p + 1) * extra] for p in range(parts)], axis=0)
        out[:, :width] = query[...]
        out[:, width : width + extra] = both.astype(BF16)
        out[:, width + extra :] = latent[...]


def open_kernel(out):
    out[...] = jnp.zeros_like(out)


def hold_kernel(value, *rest):
    out = rest[-1]
    out[:16, :128] = value[:16, :128]


def hold(value, *after):
    return pl.pallas_call(
        hold_kernel,
        out_shape=jax.ShapeDtypeStruct(value.shape, value.dtype),
        in_specs=[pl.BlockSpec(memory_space=pltpu.VMEM)] * (1 + len(after)),
        out_specs=pl.BlockSpec(memory_space=pltpu.VMEM),
        input_output_aliases={0: 0},
        compiler_params=pltpu.CompilerParams(vmem_limit_bytes=4 << 20),
    )(value, *after)


def attention_kernel(ctx, groups, heads, extra, *refs):
    pieces, (w_uk, w_uv, w_o), outs, part_ref = (
        refs[:ctx],
        refs[ctx : ctx + 3],
        refs[ctx + 3 : -1],
        refs[-1],
    )
    me, mine = lax.axis_index("ctx"), lax.axis_index(EH)
    rows = pieces[0].shape[0]
    width = NOPE + ROPE
    scale = 1.0 / math.sqrt(width)
    first = heads * width + extra
    latent = jnp.concatenate([p[:, first : first + LATENT] for p in pieces], axis=0)
    rope_keys = jnp.concatenate([p[:, first + LATENT :] for p in pieces], axis=0)
    query = jnp.concatenate([p[:, : heads * width] for p in pieces], axis=0)
    keys = jnp.dot(latent, w_uk[...], preferred_element_type=F32).astype(BF16)
    values = jnp.dot(latent, w_uv[...], preferred_element_type=F32).astype(BF16)
    total = ctx * rows

    def place(dim):
        at = lax.broadcasted_iota(jnp.int32, (total, total), dim)
        block = jnp.zeros_like(at)
        for d in range(ctx):
            here = (at >= d * rows) & (at < (d + 1) * rows)
            block = jnp.where(here, wrap(me - d, ctx) * rows - d * rows, block)
        return at + block

    allowed = place(1) <= place(0)
    contract = (((1,), (1,)), ((), ()))
    done = []
    for h in range(heads):
        q = query[:, h * width : (h + 1) * width]
        k = jnp.concatenate([keys[:, h * NOPE : (h + 1) * NOPE], rope_keys], axis=1)
        scores = lax.dot_general(q, k, contract, preferred_element_type=F32) * scale
        scores = jnp.where(allowed, scores, -1e30)
        exponent = jnp.exp(scores - jnp.max(scores, axis=1, keepdims=True))
        exponent = jnp.where(allowed, exponent, 0.0)
        weight = jnp.sum(exponent, axis=1, keepdims=True)
        summed = jnp.dot(
            exponent.astype(BF16), values[:, h * NOPE : (h + 1) * NOPE], preferred_element_type=F32
        )
        done.append((summed / weight).astype(BF16))
    partial = jnp.dot(jnp.concatenate(done, axis=1), w_o[...], preferred_element_type=F32)
    tok = rows // groups
    for n in range(ctx * groups):
        part_ref[n] = partial[n * tok : (n + 1) * tok]
    for s, out in enumerate(outs):
        to = jnp.bitwise_xor(mine, s)
        out[...] = jnp.concatenate([part_ref[d * groups + to] for d in range(ctx)], axis=0).astype(
            BF16
        )


def residual_kernel(ctx, groups, first, extra, *refs):
    sums, pieces, (travelling, kept, routes) = refs[:groups], refs[groups : groups + ctx], refs[-3:]
    me = lax.axis_index("ctx")
    tok, cols = kept.shape[1:]
    total = sums[0][...].astype(F32)
    for part in sums[1:]:
        total = total + part[...].astype(F32)
    for d in range(ctx):
        both = pieces[d][:, first : first + extra].astype(F32)
        both = jnp.concatenate(
            [both[p * tok : (p + 1) * tok] for p in range(both.shape[0] // tok)], axis=1
        )
        at = wrap(me - d, ctx)
        kept[at] = total[d * tok : (d + 1) * tok] + both[:, :cols]
        routes[at] = both[:, cols:]
    travelling[...] = jnp.concatenate([kept[b] for b in range(ctx)], axis=0).astype(BF16)


def norm_kernel(ctx, *refs):
    columns, gain, routes, out = refs[:ctx], refs[ctx], refs[ctx + 1], refs[ctx + 2]
    me = lax.axis_index("ctx")
    cols = columns[0].shape[1]
    model = ctx * cols
    values = [c[...].astype(F32) for c in columns]
    squares = values[0] * values[0]
    for v in values[1:]:
        squares = squares + v * v
    mean = jnp.sum(squares, axis=1, keepdims=True) * (1.0 / model)
    inverse = lax.rsqrt(mean + 1e-06)
    for d, v in enumerate(values):
        at = pl.ds(pl.multiple_of(wrap(me - d, ctx) * cols, 128), cols)
        out[:, at] = (v * inverse * gain[:, at]).astype(BF16)
    out[:, model:] = jnp.concatenate([routes[b] for b in range(ctx)], axis=0).astype(BF16)


def hidden_kernel(near, far, w_gate, w_up, out):
    model = w_gate.shape[1]
    rows = jnp.concatenate([near[:, :model], far[:, :model]], axis=0)
    gate_part = jnp.dot(rows, w_gate[0], preferred_element_type=F32)
    up_part = jnp.dot(rows, w_up[0], preferred_element_type=F32)
    out[...] = (gate_part / (1.0 + jnp.exp(-gate_part)) * up_part).astype(BF16)


def down(ctx, hidden, w_down):
    me = lax.axis_index("ctx")
    ff = hidden[0].shape[1]
    total = 0.0
    for d in range(ctx):
        at = pl.ds(pl.multiple_of(wrap(me - d, ctx) * ff, ff), ff)
        total = total + jnp.dot(hidden[d][...], w_down[0, at, :], preferred_element_type=F32)
    return total


def weight_of(routes, expert):
    lane = lax.broadcasted_iota(jnp.int32, routes.shape, 1)
    here = (lane == expert) | (lane == expert + 64)
    return jnp.sum(jnp.where(here, routes, 0.0), axis=1, keepdims=True)


def product_kernel(ctx, *refs):
    hidden, w_down, own_in, other_in, base = refs[:ctx], *refs[ctx : ctx + 4]
    own, other = refs[-2:]
    total = down(ctx, hidden, w_down)
    rows, model = own.shape[0], own_in.shape[1] - 128
    mine = lax.axis_index(EH)
    own_weight = weight_of(own_in[:, model:].astype(F32), mine)
    own_total = total[:rows] * own_weight
    if base.ndim == 3:
        own_total = own_total + jnp.concatenate([base[b] for b in range(ctx)], axis=0)
    own[...] = own_total
    other_weight = weight_of(other_in[:, model:].astype(F32), mine)
    other[...] = (total[rows:] * other_weight).astype(other.dtype)


def finish_kernel(ctx, own, given, started, joined, *outs):
    final = outs[-1]
    me = lax.axis_index("ctx")
    tok = outs[0].shape[0]
    total = started[...] + joined[...].astype(F32) + own[...] + given[...].astype(F32)
    for b in range(ctx):
        final[b] = total[b * tok : (b + 1) * tok]
    for d, out in enumerate(outs[:-1]):
        out[...] = final[wrap(me + d, ctx)].astype(BF16)


def gather_kernel(ctx, *refs):
    parts, out = refs[:ctx], refs[ctx]
    me = lax.axis_index("ctx")
    cols = parts[0].shape[1]
    for d, part in enumerate(parts):
        out[:, pl.ds(pl.multiple_of(wrap(me - d, ctx) * cols, 128), cols)] = part[...]


def across(value, step):
    ctx, exp = lax.axis_size("ctx"), lax.axis_size("exp")
    pairs = [
        (c * exp + e, (c + step) % ctx * exp + (e + exp // 2) % exp)
        for c in range(ctx)
        for e in range(exp)
    ]
    return lax.ppermute(value, ("ctx", "exp"), pairs)


def swap(value, step):
    size = lax.axis_size(EH)
    return lax.ppermute(value, EH, [(i, i ^ step) for i in range(size)])


def around(value, ctx):
    return [value] + [send(value, "ctx", d) for d in range(1, ctx)]


def fast_shards(
    latent, query, w_uk, w_uv, w_o, resid, norm_gain, w_gate, w_up, w_down, expert_ids, route_weights
):
    ctx, groups = lax.axis_size("ctx"), lax.axis_size(EH)
    rows, width = query.shape
    heads = width // (NOPE + ROPE)
    tok, model = resid.shape
    cols = w_o.shape[1]
    ff = w_gate.shape[2]
    extra = (cols + 128) * tok // rows
    here = ctx * tok
    like = jax.ShapeDtypeStruct

    packed = like((rows, width + extra + latent.shape[1]), BF16)
    sources = [query, latent, resid, expert_ids.T, route_weights.T]
    opened = pl.pallas_call(
        open_kernel,
        out_shape=like((8, 128), F32),
        compiler_params=pltpu.CompilerParams(vmem_limit_bytes=1 << 20),
        cost_estimate=pl.CostEstimate(flops=1 << 31, bytes_accessed=0, transcendentals=0),
    )()
    packs = call(
        functools.partial(pack_kernel, ctx, groups),
        [packed] * ctx,
        sources + [opened],
        1 << 32,
        8,
    )
    pieces = [packs[0]] + [send(packs[d], "ctx", d) for d in range(1, ctx)]
    partial = pl.pallas_call(
        functools.partial(attention_kernel, ctx, groups, heads, extra),
        out_shape=[like((here, cols), BF16)] * groups,
        in_specs=[pl.BlockSpec(memory_space=pltpu.VMEM)] * (ctx + 3),
        out_specs=[pl.BlockSpec(memory_space=pltpu.VMEM)] * groups,
        scratch_shapes=[pltpu.VMEM((ctx * groups, tok, cols), F32)],
        compiler_params=pltpu.CompilerParams(vmem_limit_bytes=16 << 20),
        cost_estimate=pl.CostEstimate(
            flops=2 * ctx * rows * heads * NOPE * (2 * LATENT + cols),
            bytes_accessed=4 << 20,
            transcendentals=heads * (ctx * rows) ** 2,
        ),
    )(*pieces, w_uk, w_uv, w_o)
    sums = [partial[0]] + [swap(partial[s], s) for s in range(1, groups)]
    travelling, kept, routes = call(
        functools.partial(residual_kernel, ctx, groups, width, extra),
        [like((here, cols), BF16), like((ctx, tok, cols), F32), like((ctx, tok, 128), F32)],
        sums + pieces,
        0,
        8,
    )
    mine = call(
        functools.partial(norm_kernel, ctx),
        like((here, model + 128), BF16),
        around(travelling, ctx) + [norm_gain.reshape(1, model), routes],
        0,
        8,
    )
    work = 4 * 2 * here * model * ff
    sibling, other = swap(mine, 1), swap(mine, groups // 2)
    hidden = call(
        hidden_kernel, like((2 * here, ff), BF16), [mine, sibling, w_gate, w_up], work, 16
    )
    near = around(hidden, ctx)
    other = hold(other, near[1])
    other_sibling = swap(other, 1)
    hidden = call(
        hidden_kernel, like((2 * here, ff), BF16), [other, other_sibling, w_gate, w_up], work, 16
    )
    far = around(hidden, ctx)
    pair = [like((here, cols), F32), like((here, cols), BF16)]
    product = functools.partial(product_kernel, ctx)
    near = call(product, pair, near + [w_down, mine, sibling, kept], work // 2, 16)
    started, joined = swap(near[0], groups // 2), swap(near[1], groups // 2 + 1)
    far = call(product, pair, far + [w_down, other, other_sibling, near[1]], work // 2, 16)
    finals = pl.pallas_call(
        functools.partial(finish_kernel, ctx),
        out_shape=[like((tok, cols), BF16)] * ctx,
        in_specs=[pl.BlockSpec(memory_space=pltpu.VMEM)] * 4,
        out_specs=[pl.BlockSpec(memory_space=pltpu.VMEM)] * ctx,
        scratch_shapes=[pltpu.VMEM((ctx, tok, cols), F32)],
        compiler_params=pltpu.CompilerParams(vmem_limit_bytes=8 << 20),
    )(far[0], swap(far[1], 1), started, joined)
    return call(
        functools.partial(gather_kernel, ctx),
        like((tok, model), BF16),
        [across(finals[d], d) for d in range(ctx)],
        0,
        8,
    )


def solution(mesh):
    placed = (
        P(("groups", "ctx"), None),
        P(("groups", "ctx"), ("exp", "head")),
        P(None, ("exp", "head")),
        P(None, ("exp", "head")),
        P(("exp", "head"), "ctx"),
        P(("groups", "ctx", "exp", "head"), None),
        P(),
        P(("exp", "head"), None, "ctx"),
        P(("exp", "head"), None, "ctx"),
        P(("exp", "head"), None, "ctx"),
        P(("groups", "ctx", "exp", "head"), None),
        P(("groups", "ctx", "exp", "head"), None),
    )
    experts = mesh.shape["exp"] * mesh.shape["head"]

    chips = mesh.shape["exp"] == 2 and mesh.shape["head"] == 2

    def step(*args):
        cols, rows = args[4].shape[1], args[1].shape[0]
        parts = rows // args[5].shape[0]
        whole = cols % 128 == 0 and (cols + 128) % (128 * parts) == 0 and parts == experts
        small = rows * mesh.shape["ctx"] <= 256
        return (fast_shards if chips and whole and small else shards)(*args)

    return jax.shard_map(
        step,
        mesh=mesh,
        in_specs=placed,
        out_specs=P(("groups", "ctx", "exp", "head"), None),
        check_vma=False,
    )
```
